256 devices in a mesh: tm: 32 (over z, y), chan: 8 (over x, core).
Axes of the slice: x: 4, y: 4, z: 8, core: 2. Of those that a mesh axis runs over, the one named last changes fastest.
Arguments:
- records: bfloat16 [512, 100, 16384], P('tm', None, 'chan'), may hold values from -6 to 6
- alive: int32 [16384], P('chan'), may hold values 0 or 1
- partner: int32 [128, 9], P('tm'), may hold values from 0 to 127, as said below
Outputs:
- stack: bfloat16 [128, 9, 16, 2, 128, 128], P('tm', None, 'chan')
The draws below stay inside these ranges and needn't reach their ends.
Inputs may be any that keep to these rules, and one draw needn't show every extreme that they name: partner[a, k] = min(a + o, 127), where o runs over the offsets 0 to 8, each once in a row; partner[a, 0] = a.
All inputs are finite; a program needn't handle non-finite values. No bound on the sum of `alive` on one device may be relied on, other than what follows from the above.
Results may differ from the reference program's by a relative error of at most 0.0052.
Values may be sent and summed in bfloat16 or wider, within the bound.
No kernel may reach another device: no remote copies, remote signals or barrier semaphores. Data moves between devices by JAX's collectives and lax.ppermute only.
A program may use at most 128 MiB of HBM per device.

```python
import math
import jax
import jax.numpy as jnp
from jax import lax

WINLEN = 100
NBIN = 16
BLOCK = 128
BAND = 8
PAIRS = 9
WIN_DEV = 16
WINDOWS = 512
NB = 128
CHANNELS = 16384


def draw_partner(key, part):
    key = jax.random.fold_in(key, 7)
    scores = jax.random.randint(key, (NB, BAND), 0, 1 << 20) * BAND + jnp.arange(BAND, dtype=jnp.int32)[None, :]
    order = jnp.argsort(scores, axis=1)
    offsets = jnp.concatenate([jnp.zeros((NB, 1), jnp.int32), order[:, :PAIRS - 1].astype(jnp.int32) + 1], axis=1)
    blocks = jnp.arange(NB, dtype=jnp.int32)[:, None]
    return jnp.minimum(blocks + offsets, NB - 1).astype(jnp.int32)


def set_ends(values, stream_key, smallest, top_value):
    shape = values.shape
    index_at = [jax.random.randint(jax.random.fold_in(stream_key, axis), (), 0, shape[axis]) for axis in range(len(shape))]
    values = values.at[tuple(index_at)].set(smallest)
    longest = shape.index(max(shape))
    index_at[longest] = (index_at[longest] + 1) % shape[longest]
    return values.at[tuple(index_at)].set(top_value)


def level_of(key, shape, pieces, smallest, top_value):
    level = 1.0
    for dim, shards_of in pieces:
        draws = jax.random.uniform(jax.random.fold_in(jax.random.fold_in(key, 6), dim), (shards_of,), jnp.float32, smallest / len(pieces), top_value / len(pieces))
        level = level * jnp.repeat(jnp.exp(draws), shape[dim] // shards_of).reshape((-1,) + (1,) * (len(shape) - 1 - dim))
    return level


def gaussian(stream_key, shape, width, bound, cuts=(), kind=jnp.bfloat16):
    entries = jax.random.normal(stream_key, shape, jnp.float32) * width
    if len(cuts) > 0:
        entries = level_of(stream_key, shape, cuts, -0.22, 0.18) * entries
    return jnp.clip(entries, min=-bound, max=bound).astype(kind)


def setup_inputs(seed: int = 0) -> dict:
    seeds = jax.random.split(jax.random.key(seed), 4)
    records = gaussian(seeds[0], (WINDOWS, WINLEN, CHANNELS), 1.0, 6.0, ((0, 32), (2, 8)))
    alive = set_ends((jax.random.randint(seeds[1], (CHANNELS,), 0, 8) < 7).astype(jnp.int32), jax.random.fold_in(seeds[1], 1), 0, 1)
    partner = draw_partner(jax.random.fold_in(seeds[3], 71), 0)
    return dict(records=records, alive=alive, partner=partner)


def dft_table(length, count):
    samples = jnp.arange(length, dtype=jnp.float32)
    freqs = jnp.arange(count, dtype=jnp.float32) + 4.0
    angle = 2.0 * jnp.pi * freqs[:, None] * samples[None, :] / length
    factor = jnp.sqrt(jnp.float32(2.0) / length)
    return jnp.stack([jnp.cos(angle) * factor, -jnp.sin(angle) * factor], axis=1)

def reference(records, alive, partner):
    table = dft_table(WINLEN, NBIN)
    live = alive.astype(jnp.float32)

    def transform(group):
        signal = group.astype(jnp.float32)
        power = lax.optimization_barrier(jnp.mean(signal * signal, axis=1, keepdims=True))
        normed = signal / jnp.sqrt(power + 1e-05) * live[None, None, :]
        return jnp.einsum('fpt,wtc->wfpc', table, normed, precision=lax.Precision.HIGHEST).astype(jnp.bfloat16)
    grouped = records.reshape(WINDOWS // WIN_DEV, WIN_DEV, WINLEN, CHANNELS)
    spectra = lax.map(transform, grouped).reshape(WINDOWS, NBIN, 2, NB, BLOCK)
    inverse = 1.0 / math.sqrt(WINDOWS)

    def one_block(index):
        own = lax.dynamic_index_in_dim(spectra, index, 3, keepdims=False).astype(jnp.float32)
        others = jnp.take(spectra, partner[index], axis=3).astype(jnp.float32)
        product = jnp.einsum('wfpi,wfqkj->kfpqij', own, others)
        real_part = product[:, :, 0, 0] + product[:, :, 1, 1]
        imag_part = product[:, :, 0, 1] - product[:, :, 1, 0]
        return (jnp.stack([real_part, imag_part], axis=2) * inverse).astype(jnp.bfloat16)
    return lax.map(one_block, jnp.arange(NB, dtype=jnp.int32))
```

```python
import math

import jax
import jax.numpy as jnp
import numpy as np
from jax import lax
from jax.experimental import pallas as pl
from jax.experimental.pallas import tpu as pltpu
from jax.sharding import PartitionSpec as P

WINLEN = 100
NBIN = 16
BLOCK = 128
WIN_DEV = 16
WINDOWS = 512
PAIRS = 9
NZ, NY, NC = 8, 4, 8
NF = 2
GROUP = 4
REACH = 12
COLS = 256
BOTH = ("tm", "chan")


def dft_rows():
    t = np.arange(WINLEN)
    bins = np.arange(NBIN) + 4
    angle = 2.0 * np.pi * bins[:, None] * t[None, :] / WINLEN
    table = np.stack([np.cos(angle), -np.sin(angle)], axis=1) * math.sqrt(2.0 / WINLEN)
    high = table.astype(jnp.bfloat16)
    low = (table - high.astype(np.float64)).astype(jnp.bfloat16)
    parts = np.stack([high, low]).astype(np.float32).reshape(2, NC, NF, 2, WINLEN)
    parts = parts.transpose(1, 0, 2, 3, 4)
    rows = parts[:, :, :, :, None, :, None] * np.eye(WIN_DEV, dtype=np.float32)[:, None, :]
    return rows.reshape(NC, 2 * NF * 2 * WIN_DEV, WINLEN * WIN_DEV).astype(jnp.bfloat16)


def spectra_kernel(order, records, alive, *refs):
    rows, outs = refs[:NC], refs[NC:]
    x = records[...]
    signal = x.astype(jnp.float32)
    power = jnp.sum(signal * signal, axis=0) * (1.0 / WINLEN)
    scale = alive[...].astype(jnp.float32) / jnp.sqrt(power + 1e-05)
    x = x.reshape(WINLEN * WIN_DEV, COLS)
    lhs = jnp.concatenate([r[0] for r in rows], axis=0)
    y = jnp.dot(lhs, x, preferred_element_type=jnp.float32)
    half = NF * 2 * WIN_DEV
    for k in range(NC):
        at = 2 * half * k
        value = y[at : at + half] + y[at + half : at + 2 * half]
        for f in range(NF):
            for p in range(2):
                row = (f * 2 + p) * WIN_DEV
                scaled = (value[row : row + WIN_DEV] * scale).astype(jnp.bfloat16)
                for b in range(COLS // BLOCK):
                    outs[f * NC + k][b, p] = scaled[:, b * BLOCK : (b + 1) * BLOCK]


def spectra_slots(records, alive, order):
    channels = records.shape[2]
    blocks = channels // BLOCK
    rows = jnp.asarray(dft_rows())
    per = COLS // BLOCK
    grid_spec = pltpu.PrefetchScalarGridSpec(
        num_scalar_prefetch=1,
        grid=(channels // COLS,),
        in_specs=[
            pl.BlockSpec((WINLEN, WIN_DEV, COLS), lambda n, o: (0, 0, n)),
            pl.BlockSpec((1, COLS), lambda n, o: (0, n)),
        ]
        + [pl.BlockSpec((1,) + rows.shape[1:], lambda n, o, k=k: (o[k], 0, 0)) for k in range(NC)],
        out_specs=[pl.BlockSpec((per, 2, WIN_DEV, BLOCK), lambda n, o: (n, 0, 0, 0))] * (NF * NC),
    )
    return pl.pallas_call(
        spectra_kernel,
        grid_spec=grid_spec,
        out_shape=[jax.ShapeDtypeStruct((blocks, 2, WIN_DEV, BLOCK), jnp.bfloat16)] * (NF * NC),
        compiler_params=pltpu.CompilerParams(vmem_limit_bytes=40 << 20),
        name="spectra",
    )(order, records, alive, *([rows] * NC))


def pack_kernel(place, *refs):
    slots, halo, outs = refs[:NC], refs[NC], refs[NC + 1 :]
    y = place[0]
    for k in range(NY):
        target = lax.rem(y + k, NY)
        for i in range(3):
            group = target + i

            @pl.when(group < NY)
            def _():
                for s in range(NC):
                    outs[k][s, i] = slots[s][group]

            @pl.when(group >= NY)
            def _():
                for s in range(NC):
                    outs[k][s, i] = halo[s, group - NY]


def pack(place, slots, halo):
    vmem = pl.BlockSpec(memory_space=pltpu.VMEM)
    shape = jax.ShapeDtypeStruct((NC, 3, GROUP, 2, WIN_DEV, BLOCK), jnp.bfloat16)
    return pl.pallas_call(
        pack_kernel,
        in_specs=[pl.BlockSpec(memory_space=pltpu.SMEM)] + [vmem] * (NC + 1),
        out_specs=[vmem] * NY,
        out_shape=[shape] * NY,
        compiler_params=pltpu.CompilerParams(vmem_limit_bytes=16 << 20),
        name="pack",
    )(place, *slots, halo)


def block_of(refs, index):
    pieces = []
    for ref in refs:
        value = ref[:, index]
        halves = [value[:, p].reshape(NC * WIN_DEV, BLOCK) for p in range(2)]
        pieces.append(jnp.concatenate(halves, axis=1))
    return jnp.concatenate(pieces, axis=0)


def stack_kernel(relative, *refs):
    spectra, out, own_t = refs[:NY], refs[-2], refs[-1]
    a = pl.program_id(0)
    own_t[...] = block_of(spectra, a).T
    for k in range(PAIRS):
        other = block_of(spectra, relative[a, k])
        product = jnp.dot(own_t[...], other, preferred_element_type=jnp.float32)
        real = product[:BLOCK, :BLOCK] + product[BLOCK:, BLOCK:]
        imag = product[:BLOCK, BLOCK:] - product[BLOCK:, :BLOCK]
        inverse = 1.0 / math.sqrt(WINDOWS)
        out[0, k, 0, 0] = (real * inverse).astype(jnp.bfloat16)
        out[0, k, 0, 1] = (imag * inverse).astype(jnp.bfloat16)


def stacks(relative, spectra, f, earlier=None):
    shape = (GROUP, PAIRS, NF, 2, BLOCK, BLOCK)
    whole = pl.BlockSpec((NC, REACH, 2, WIN_DEV, BLOCK), lambda a, r: (0, 0, 0, 0, 0))
    args = [s.reshape(NC, REACH, 2, WIN_DEV, BLOCK) for s in spectra]
    specs = [whole] * NY
    aliases = {}
    if earlier is not None:
        args.append(earlier)
        specs.append(pl.BlockSpec(memory_space=pl.ANY))
        aliases = {1 + NY: 0}
    grid_spec = pltpu.PrefetchScalarGridSpec(
        num_scalar_prefetch=1,
        grid=(GROUP,),
        in_specs=specs,
        out_specs=pl.BlockSpec((1, PAIRS, 1, 2, BLOCK, BLOCK), lambda a, r: (a, 0, f, 0, 0, 0)),
        scratch_shapes=[pltpu.VMEM((2 * BLOCK, WINDOWS), jnp.bfloat16)],
    )
    return pl.pallas_call(
        stack_kernel,
        grid_spec=grid_spec,
        out_shape=jax.ShapeDtypeStruct(shape, jnp.bfloat16),
        input_output_aliases=aliases,
        compiler_params=pltpu.CompilerParams(vmem_limit_bytes=24 << 20),
        name="stacks",
    )(relative, *args)


def slot_route(k):
    route = []
    for z in range(NZ):
        for y in range(NY):
            for c in range(NC):
                route.append(((z * NY + y) * NC + c, (c * NY + y) * NC + (c + z + k) % NC))
    return route


def per_device(records, alive, partner):
    tm, chan = lax.axis_index("tm"), lax.axis_index("chan")
    z, y = tm // NY, tm % NY
    order = (chan + z + jnp.arange(NC, dtype=jnp.int32)) % NC
    sent = spectra_slots(jnp.transpose(records, (1, 0, 2)), alive.reshape(1, -1), order)
    place = y.reshape(1).astype(jnp.int32)
    relative = partner - tm * GROUP
    down = [(i, i - NY) for i in range(NY, NZ * NY)]
    result = None
    for f in range(NF):
        slots = [lax.ppermute(sent[f * NC + k], BOTH, slot_route(k)) for k in range(NC)]
        slots = [s.reshape(NY, GROUP, 2, WIN_DEV, BLOCK) for s in slots]
        halo = lax.ppermute(jnp.stack([slots[(k - 1) % NC][:2] for k in range(NC)]), "tm", down)
        packed = pack(place, slots, halo)
        spectra = [packed[0]]
        for k in range(1, NY):
            route = [(i, i // NY * NY + (i + k) % NY) for i in range(NZ * NY)]
            spectra.append(lax.ppermute(packed[k], "tm", route))
        result = stacks(relative, spectra, f, result)
    return result


def solution(mesh):
    return jax.shard_map(
        per_device,
        mesh=mesh,
        in_specs=(P("tm", None, "chan"), P("chan"), P("tm", None)),
        out_specs=P("tm", None, "chan", None, None, None),
        check_vma=False,
    )
```

```python
import functools
import math

import jax
import jax.numpy as jnp
import numpy as np
from jax import lax
from jax.experimental import pallas as pl
from jax.experimental.pallas import tpu as pltpu
from jax.sharding import PartitionSpec as P

WINLEN = 100
NBIN = 16
BLOCK = 128
WIN_DEV = 16
WINDOWS = 512
PAIRS = 9
NZ, NY, NC = 8, 4, 8
NF = 2
GROUP = 4
REACH = 12
COLS = 512


def dft_rows():
    t = np.arange(WINLEN)
    bins = np.arange(NBIN) + 4
    angle = 2.0 * np.pi * bins[:, None] * t[None, :] / WINLEN
    table = np.stack([np.cos(angle), -np.sin(angle)], axis=1) * math.sqrt(2.0 / WINLEN)
    high = table.astype(jnp.bfloat16)
    low = (table - high.astype(np.float64)).astype(jnp.bfloat16)
    parts = np.stack([high, low]).astype(np.float32).reshape(2, NC, NF, 2, WINLEN)
    parts = parts.transpose(2, 1, 0, 3, 4)
    rows = parts[:, :, :, :, None, :, None] * np.eye(WIN_DEV, dtype=np.float32)[:, None, :]
    return rows.reshape(NF, NC, 4 * WIN_DEV, WINLEN * WIN_DEV).astype(jnp.bfloat16)


def spectra_kernel(order, records, alive, *refs):
    rows, outs = refs[:NC], refs[NC:]
    x = records[...]
    signal = x.astype(jnp.float32)
    power = jnp.sum(signal * signal, axis=0) * (1.0 / WINLEN)
    scale = alive[...].astype(jnp.float32) / jnp.sqrt(power + 1e-05)
    x = x.reshape(WINLEN * WIN_DEV, COLS)
    lhs = jnp.concatenate([r[0, 0] for r in rows], axis=0)
    y = jnp.dot(lhs, x, preferred_element_type=jnp.float32)
    for k in range(NC):
        at = 4 * WIN_DEV * k
        value = y[at : at + 2 * WIN_DEV] + y[at + 2 * WIN_DEV : at + 4 * WIN_DEV]
        for p in range(2):
            scaled = (value[p * WIN_DEV : (p + 1) * WIN_DEV] * scale).astype(jnp.bfloat16)
            for b in range(COLS // BLOCK):
                part = scaled[:, b * BLOCK : (b + 1) * BLOCK]
                if len(outs) == NC:
                    outs[k][b, p] = part
                else:
                    outs[0][k, b, p] = part


def spectra_of(f, records, alive, rows, order, apart):
    channels = records.shape[2]
    blocks = channels // BLOCK
    per = COLS // BLOCK
    if apart:
        shape = [jax.ShapeDtypeStruct((blocks, 2, WIN_DEV, BLOCK), jnp.bfloat16)] * NC
        out_specs = [pl.BlockSpec((per, 2, WIN_DEV, BLOCK), lambda n, o: (n, 0, 0, 0))] * NC
    else:
        shape = jax.ShapeDtypeStruct((NC, blocks, 2, WIN_DEV, BLOCK), jnp.bfloat16)
        out_specs = pl.BlockSpec((NC, per, 2, WIN_DEV, BLOCK), lambda n, o: (0, n, 0, 0, 0))
    grid_spec = pltpu.PrefetchScalarGridSpec(
        num_scalar_prefetch=1,
        grid=(channels // COLS,),
        in_specs=[
            pl.BlockSpec((WINLEN, WIN_DEV, COLS), lambda n, o: (0, 0, n)),
            pl.BlockSpec((1, COLS), lambda n, o: (0, n)),
        ]
        + [pl.BlockSpec((1, 1) + rows.shape[2:], lambda n, o, k=k: (f, o[k], 0, 0)) for k in range(NC)],
        out_specs=out_specs,
    )
    return pl.pallas_call(
        spectra_kernel,
        grid_spec=grid_spec,
        out_shape=shape,
        compiler_params=pltpu.CompilerParams(vmem_limit_bytes=60 << 20),
        name="spectra",
    )(order, records, alive, *([rows] * NC))


def arrange_kernel(order, *refs):
    for k in range(NC):
        refs[NC][order[k]] = refs[k][...]


def arrange(order, slots):
    vmem = pl.BlockSpec(memory_space=pltpu.VMEM)
    return pl.pallas_call(
        arrange_kernel,
        in_specs=[pl.BlockSpec(memory_space=pltpu.SMEM)] + [vmem] * NC,
        out_specs=vmem,
        out_shape=jax.ShapeDtypeStruct((NC,) + slots[0].shape, jnp.bfloat16),
        compiler_params=pltpu.CompilerParams(vmem_limit_bytes=16 << 20),
        name="arrange",
    )(order, *slots)


def pack_kernel(first, count, place, *refs):
    planes, halo, outs = refs[0], refs[1], refs[-NY:]
    y = place[0]
    for k in range(NY):
        target = lax.rem(y + k, NY)
        for i in range(count):
            group = target + first + i
            if first == 0:
                outs[k][:, i] = planes[:, group]
            else:

                @pl.when(group < NY)
                def _():
                    outs[k][:, i] = planes[:, group]

                @pl.when(group >= NY)
                def _():
                    outs[k][:, i] = halo[:, group - NY]


def pack(place, first, count, *sources):
    vmem = pl.BlockSpec(memory_space=pltpu.VMEM)
    shape = jax.ShapeDtypeStruct((NZ, count, GROUP, 2, WIN_DEV, BLOCK), jnp.bfloat16)
    return pl.pallas_call(
        functools.partial(pack_kernel, first, count),
        in_specs=[pl.BlockSpec(memory_space=pltpu.SMEM)] + [vmem] * len(sources),
        out_specs=[vmem] * NY,
        out_shape=[shape] * NY,
        compiler_params=pltpu.CompilerParams(vmem_limit_bytes=16 << 20),
        name="pack",
    )(place, *sources)


def stack_kernel(relative, *refs):
    near, far, out, window, own_t = refs[:NY], refs[NY : 2 * NY], refs[-3], refs[-2], refs[-1]
    a = pl.program_id(0)
    rows = NZ * WIN_DEV

    @pl.when(a == 0)
    def _():
        for y in range(NY):
            for b in range(REACH):
                for p in range(2):
                    ref, at = (near[y], b) if b < GROUP else (far[y], b - GROUP)
                    tile = ref[:, at // GROUP, at % GROUP, p].reshape(rows, BLOCK)
                    window[b, y * rows : (y + 1) * rows, p * BLOCK : (p + 1) * BLOCK] = tile

    own_t[...] = window[a].T
    for k in range(PAIRS):
        other = window[relative[a, k]]
        product = jnp.dot(own_t[...], other, preferred_element_type=jnp.float32)
        real = product[:BLOCK, :BLOCK] + product[BLOCK:, BLOCK:]
        imag = product[:BLOCK, BLOCK:] - product[BLOCK:, :BLOCK]
        inverse = 1.0 / math.sqrt(WINDOWS)
        out[0, k, 0, 0] = (real * inverse).astype(jnp.bfloat16)
        out[0, k, 0, 1] = (imag * inverse).astype(jnp.bfloat16)


def stacks(relative, near, far, f, earlier=None):
    shape = (GROUP, PAIRS, NF, 2, BLOCK, BLOCK)
    args = [*near, *far]
    specs = [pl.BlockSpec(s.shape, lambda a, r: (0,) * 6) for s in args]
    aliases = {}
    if earlier is not None:
        aliases = {1 + len(args): 0}
        args.append(earlier)
        specs.append(pl.BlockSpec(memory_space=pl.ANY))
    grid_spec = pltpu.PrefetchScalarGridSpec(
        num_scalar_prefetch=1,
        grid=(GROUP,),
        in_specs=specs,
        out_specs=pl.BlockSpec((1, PAIRS, 1, 2, BLOCK, BLOCK), lambda a, r: (a, 0, f, 0, 0, 0)),
        scratch_shapes=[
            pltpu.VMEM((REACH, WINDOWS, 2 * BLOCK), jnp.bfloat16),
            pltpu.VMEM((2 * BLOCK, WINDOWS), jnp.bfloat16),
        ],
    )
    return pl.pallas_call(
        stack_kernel,
        grid_spec=grid_spec,
        out_shape=jax.ShapeDtypeStruct(shape, jnp.bfloat16),
        input_output_aliases=aliases,
        compiler_params=pltpu.CompilerParams(vmem_limit_bytes=24 << 20),
        name="stacks",
    )(relative, *args)


def per_device(records, alive, partner):
    tm = lax.axis_index("tm")
    place = (tm % NY).reshape(1).astype(jnp.int32)
    relative = partner - tm * GROUP
    rows = jnp.asarray(dft_rows())
    records, alive = jnp.transpose(records, (1, 0, 2)), alive.reshape(1, -1)
    columns = [[z * NY + y for z in range(NZ)] for y in range(NY)]
    down = [(i, i - NY) for i in range(NY, NZ * NY)]
    rounds = [[(i, i // NY * NY + (i + k) % NY) for i in range(NZ * NY)] for k in range(NY)]

    def along_y(packed):
        return [packed[0]] + [lax.ppermute(packed[k], "tm", rounds[k]) for k in range(1, NY)]

    def across_z(sent):
        planes = lax.all_to_all(
            sent, "tm", split_axis=0, concat_axis=0, tiled=True, axis_index_groups=columns
        )
        return planes.reshape(NZ, NY, GROUP, 2, WIN_DEV, BLOCK)

    def halo_of(planes):
        return lax.ppermute(planes[:, :2], "tm", down)

    barrier = lax.optimization_barrier
    plain = jnp.arange(NC, dtype=jnp.int32)
    mixed = jnp.bitwise_xor(plain, lax.axis_index("chan").astype(jnp.int32))
    own0 = spectra_of(0, records, alive, rows, plain, False)
    own1 = spectra_of(1, records, alive, rows, mixed, True)
    sent0 = lax.all_to_all(own0, "chan", split_axis=0, concat_axis=0, tiled=True)
    sent0, own1 = barrier((sent0, own1))
    planes0 = across_z(sent0)
    slots1 = [own1[0]]
    for k in range(1, NC):
        slots1.append(lax.ppermute(own1[k], "chan", [(c, c ^ k) for c in range(NC)]))
    planes0, slots1 = barrier((planes0, slots1))
    near0 = along_y(pack(place, 0, 1, planes0))
    far0 = pack(place, 1, 2, planes0, halo_of(planes0))
    sent1 = arrange(mixed, slots1)
    sent1, near0, far0 = barrier((sent1, near0, far0))
    far0 = along_y(far0)
    planes1 = across_z(sent1)
    planes1, near0, far0 = barrier((planes1, near0, far0))
    halo1 = halo_of(planes1)
    near1 = along_y(pack(place, 0, 1, planes1))
    halo1, near1 = barrier((halo1, near1))
    far1 = along_y(pack(place, 1, 2, planes1, halo1))
    result = stacks(relative, near0, far0, 0)
    return stacks(relative, near1, far1, 1, result)


def solution(mesh):
    return jax.shard_map(
        per_device,
        mesh=mesh,
        in_specs=(P("tm", None, "chan"), P("chan"), P("tm", None)),
        out_specs=P("tm", None, "chan", None, None, None),
        check_vma=False,
    )
```

```python
import functools
import math

import jax
import jax.numpy as jnp
import numpy as np
from jax import lax
from jax.experimental import pallas as pl
from jax.experimental.pallas import tpu as pltpu
from jax.sharding import PartitionSpec as P

WINLEN = 100
NBIN = 16
BLOCK = 128
WIN_DEV = 16
WINDOWS = 512
PAIRS = 9
NZ, NY, NC = 8, 4, 8
NF = 2
GROUP = 4
REACH = 12
COLS = 512


def dft_rows():
    t = np.arange(WINLEN)
    bins = np.arange(NBIN) + 4
    angle = 2.0 * np.pi * bins[:, None] * t[None, :] / WINLEN
    table = np.stack([np.cos(angle), -np.sin(angle)], axis=1) * math.sqrt(2.0 / WINLEN)
    high = table.astype(jnp.bfloat16)
    low = (table - high.astype(np.float64)).astype(jnp.bfloat16)
    parts = np.stack([high, low]).astype(np.float32).reshape(2, NC, NF, 2, WINLEN)
    parts = parts.transpose(2, 1, 0, 3, 4)
    rows = parts[:, :, :, :, None, :, None] * np.eye(WIN_DEV, dtype=np.float32)[:, None, :]
    return rows.reshape(NF, NC, 4 * WIN_DEV, WINLEN * WIN_DEV).astype(jnp.bfloat16)


def spectra_body(records, alive, lhs, store):
    x = records[...]
    signal = x.astype(jnp.float32)
    power = jnp.sum(signal * signal, axis=0) * (1.0 / WINLEN)
    scale = alive[...].astype(jnp.float32) / jnp.sqrt(power + 1e-05)
    x = x.reshape(WINLEN * WIN_DEV, COLS)
    y = jnp.dot(lhs, x, preferred_element_type=jnp.float32)
    for k in range(NC):
        at = 4 * WIN_DEV * k
        value = y[at : at + 2 * WIN_DEV] + y[at + 2 * WIN_DEV : at + 4 * WIN_DEV]
        for p in range(2):
            scaled = (value[p * WIN_DEV : (p + 1) * WIN_DEV] * scale).astype(jnp.bfloat16)
            for b in range(COLS // BLOCK):
                store(k, b, p, scaled[:, b * BLOCK : (b + 1) * BLOCK])


def spectra_kernel(records, alive, rows, out):
    def store(k, b, p, part):
        out[k, b, p] = part

    spectra_body(records, alive, rows[0].reshape(NC * 4 * WIN_DEV, WINLEN * WIN_DEV), store)


def spectra_of(f, records, alive, rows):
    channels = records.shape[2]
    blocks, per = channels // BLOCK, COLS // BLOCK
    return pl.pallas_call(
        spectra_kernel,
        grid=(channels // COLS,),
        in_specs=[
            pl.BlockSpec((WINLEN, WIN_DEV, COLS), lambda n: (0, 0, n)),
            pl.BlockSpec((1, COLS), lambda n: (0, n)),
            pl.BlockSpec((1,) + rows.shape[1:], lambda n: (f, 0, 0, 0)),
        ],
        out_specs=pl.BlockSpec((NC, per, 2, WIN_DEV, BLOCK), lambda n: (0, n, 0, 0, 0)),
        out_shape=jax.ShapeDtypeStruct((NC, blocks, 2, WIN_DEV, BLOCK), jnp.bfloat16),
        compiler_params=pltpu.CompilerParams(vmem_limit_bytes=60 << 20),
        name="spectra",
    )(records, alive, rows)


def spectra_apart_kernel(order, records, alive, *refs):
    rows, outs = refs[:NC], refs[NC:]

    def store(k, b, p, part):
        outs[k][b, p] = part

    spectra_body(records, alive, jnp.concatenate([r[0, 0] for r in rows], axis=0), store)


def spectra_apart(f, records, alive, rows, order):
    channels = records.shape[2]
    blocks, per = channels // BLOCK, COLS // BLOCK
    grid_spec = pltpu.PrefetchScalarGridSpec(
        num_scalar_prefetch=1,
        grid=(channels // COLS,),
        in_specs=[
            pl.BlockSpec((WINLEN, WIN_DEV, COLS), lambda n, o: (0, 0, n)),
            pl.BlockSpec((1, COLS), lambda n, o: (0, n)),
        ]
        + [pl.BlockSpec((1, 1) + rows.shape[2:], lambda n, o, k=k: (f, o[k], 0, 0)) for k in range(NC)],
        out_specs=[pl.BlockSpec((per, 2, WIN_DEV, BLOCK), lambda n, o: (n, 0, 0, 0))] * NC,
    )
    return pl.pallas_call(
        spectra_apart_kernel,
        grid_spec=grid_spec,
        out_shape=[jax.ShapeDtypeStruct((blocks, 2, WIN_DEV, BLOCK), jnp.bfloat16)] * NC,
        compiler_params=pltpu.CompilerParams(vmem_limit_bytes=60 << 20),
        name="spectra",
    )(order, records, alive, *([rows] * NC))


def place_plane(out, plane, value):
    out[plane, :NY] = value
    out[lax.rem(plane + NZ - 1, NZ), NY:] = value[:2]


def widen_kernel(planes, out):
    for k in range(NZ):
        place_plane(out, k, planes[k])


def widen(planes):
    vmem = pl.BlockSpec(memory_space=pltpu.VMEM)
    return pl.pallas_call(
        widen_kernel,
        in_specs=[vmem],
        out_specs=vmem,
        out_shape=jax.ShapeDtypeStruct((NZ, NY + 2, GROUP, 2, WIN_DEV, BLOCK), jnp.bfloat16),
        compiler_params=pltpu.CompilerParams(vmem_limit_bytes=16 << 20),
        name="widen",
    )(planes.reshape(NZ, NY, GROUP, 2, WIN_DEV, BLOCK))


def arrange_kernel(order, *refs):
    for k in range(NC):
        refs[NC][order[k]] = refs[k][...]


def arrange(order, slots):
    vmem = pl.BlockSpec(memory_space=pltpu.VMEM)
    return pl.pallas_call(
        arrange_kernel,
        in_specs=[pl.BlockSpec(memory_space=pltpu.SMEM)] + [vmem] * NC,
        out_specs=vmem,
        out_shape=jax.ShapeDtypeStruct((NC,) + slots[0].shape, jnp.bfloat16),
        compiler_params=pltpu.CompilerParams(vmem_limit_bytes=16 << 20),
        name="arrange",
    )(order, *slots)


def pack_kernel(place, planes, *outs):
    for k in range(NY):
        outs[k][...] = planes[:, pl.ds(lax.rem(place[0] + k, NY), 3)]


def pack(place, planes):
    vmem = pl.BlockSpec(memory_space=pltpu.VMEM)
    shape = jax.ShapeDtypeStruct((NZ, 3, GROUP, 2, WIN_DEV, BLOCK), jnp.bfloat16)
    return pl.pallas_call(
        pack_kernel,
        in_specs=[pl.BlockSpec(memory_space=pltpu.SMEM), vmem],
        out_specs=[vmem] * NY,
        out_shape=[shape] * NY,
        compiler_params=pltpu.CompilerParams(vmem_limit_bytes=16 << 20),
        name="pack",
    )(place, planes)


def pack_group_kernel(first, place, planes, *refs):
    halo, outs = (None, refs) if first == 0 else (refs[0], refs[1:])
    for n, out in enumerate(outs):
        group = lax.rem(place[0] + n % NY, NY) + max(first, 0) + n // NY
        if first == 0:
            out[...] = planes[:, group]
        else:

            @pl.when(group < NY)
            def _():
                out[...] = planes[:, group]

            @pl.when(group >= NY)
            def _():
                out[...] = halo[:, group - NY]


def pack_groups(place, first, count, *sources):
    vmem = pl.BlockSpec(memory_space=pltpu.VMEM)
    shape = jax.ShapeDtypeStruct((NZ, GROUP, 2, WIN_DEV, BLOCK), jnp.bfloat16)
    return pl.pallas_call(
        functools.partial(pack_group_kernel, first),
        in_specs=[pl.BlockSpec(memory_space=pltpu.SMEM)] + [vmem] * len(sources),
        out_specs=[vmem] * (NY * count),
        out_shape=[shape] * (NY * count),
        compiler_params=pltpu.CompilerParams(vmem_limit_bytes=16 << 20),
        name="pack",
    )(place, *sources)


def real_and_imag(product):
    real = product[:BLOCK, :BLOCK] + product[BLOCK:, BLOCK:]
    imag = product[:BLOCK, BLOCK:] - product[BLOCK:, :BLOCK]
    inverse = 1.0 / math.sqrt(WINDOWS)
    return (real * inverse).astype(jnp.bfloat16), (imag * inverse).astype(jnp.bfloat16)


def fill(window, at, tiles, y, p):
    rows = NZ * WIN_DEV
    window[at, y * rows : (y + 1) * rows, p * BLOCK : (p + 1) * BLOCK] = tiles.reshape(rows, BLOCK)


def stack_kernel(held, relative, *refs):
    sources, out, window, own_t = refs[:-3], refs[-3], refs[-2], refs[-1]
    a = pl.program_id(0)

    @pl.when(a == 0)
    def _():
        for y in range(NY):
            for b in range(held):
                for p in range(2):
                    if sources[0].ndim == 6:
                        tiles = sources[y][:, b // GROUP, b % GROUP, p]
                    else:
                        tiles = sources[b // GROUP * NY + y][:, b % GROUP, p]
                    fill(window, b, tiles, y, p)

    own_t[...] = window[a].T
    for k in range(PAIRS):
        other = window[jnp.minimum(relative[a, k], held - 1)]
        product = jnp.dot(own_t[...], other, preferred_element_type=jnp.float32)
        out[0, k, 0, 0], out[0, k, 0, 1] = real_and_imag(product)


def stacks(relative, sources, f, held, earlier=None):
    shape = (GROUP, PAIRS, NF, 2, BLOCK, BLOCK)
    args = list(sources)
    specs = [pl.BlockSpec(memory_space=pltpu.VMEM)] * len(args)
    aliases = {}
    kernel = functools.partial(stack_kernel, held)
    if earlier is not None:
        aliases = {1 + len(args): 0}
        args.append(earlier)
        specs.append(pl.BlockSpec(memory_space=pl.ANY))

        def kernel(relative, *refs):
            stack_kernel(held, relative, *refs[:-4], *refs[-3:])

    grid_spec = pltpu.PrefetchScalarGridSpec(
        num_scalar_prefetch=1,
        grid=(GROUP,),
        in_specs=specs,
        out_specs=pl.BlockSpec((1, PAIRS, 1, 2, BLOCK, BLOCK), lambda a, r: (a, 0, f, 0, 0, 0)),
        scratch_shapes=[
            pltpu.VMEM((held, WINDOWS, 2 * BLOCK), jnp.bfloat16),
            pltpu.VMEM((2 * BLOCK, WINDOWS), jnp.bfloat16),
        ],
    )
    return pl.pallas_call(
        kernel,
        grid_spec=grid_spec,
        out_shape=jax.ShapeDtypeStruct(shape, jnp.bfloat16),
        input_output_aliases=aliases,
        compiler_params=pltpu.CompilerParams(vmem_limit_bytes=20 << 20),
        name="stacks",
    )(relative, *args)


def last_kernel(f, relative, *refs):
    near, last, out = refs[:NY], refs[NY : 2 * NY], refs[2 * NY + 1]
    window, own, staged, sems = refs[2 * NY + 2 :]
    for y in range(NY):
        for b in range(GROUP):
            for p in range(2):
                fill(own, b, near[y][:, b, p], y, p)
                fill(window, b, last[y][:, b, p], y, p)

    def each(step):
        for a in range(GROUP):
            for k in range(PAIRS):
                far = relative[a, k] - 2 * GROUP

                @pl.when(far >= 0)
                def _():
                    step(pltpu.make_async_copy(staged.at[a, far], out.at[a, k, f], sems.at[a, k]))

    for a in range(GROUP):
        own_t = own[a].T
        for b in range(a + 1):
            product = jnp.dot(own_t, window[b], preferred_element_type=jnp.float32)
            staged[a, b, 0], staged[a, b, 1] = real_and_imag(product)
    each(lambda copy: copy.start())
    each(lambda copy: copy.wait())


def last_stacks(relative, near, last, f, earlier):
    vmem = pl.BlockSpec(memory_space=pltpu.VMEM)
    blocks = pltpu.VMEM((GROUP, WINDOWS, 2 * BLOCK), jnp.bfloat16)
    return pl.pallas_call(
        functools.partial(last_kernel, f),
        in_specs=[pl.BlockSpec(memory_space=pltpu.SMEM)]
        + [vmem] * (2 * NY)
        + [pl.BlockSpec(memory_space=pl.ANY)],
        out_specs=pl.BlockSpec(memory_space=pl.ANY),
        out_shape=jax.ShapeDtypeStruct(earlier.shape, earlier.dtype),
        input_output_aliases={1 + 2 * NY: 0},
        scratch_shapes=[
            blocks,
            blocks,
            pltpu.VMEM((GROUP, GROUP, 2, BLOCK, BLOCK), jnp.bfloat16),
            pltpu.SemaphoreType.DMA((GROUP, PAIRS)),
        ],
        compiler_params=pltpu.CompilerParams(vmem_limit_bytes=20 << 20),
        name="last_stacks",
    )(relative, *near, *last, earlier)


def per_device(records, alive, partner):
    tm = lax.axis_index("tm")
    place = (tm % NY).reshape(1).astype(jnp.int32)
    relative = partner - tm * GROUP
    rows = jnp.asarray(dft_rows())
    records, alive = jnp.transpose(records, (1, 0, 2)), alive.reshape(1, -1)
    columns = [[z * NY + y for z in range(NZ)] for y in range(NY)]
    rounds = [[(i, i // NY * NY + (i + k) % NY) for i in range(NZ * NY)] for k in range(NY)]

    def along_y(packed):
        return [packed[0]] + [lax.ppermute(packed[k], "tm", rounds[k]) for k in range(1, NY)]

    def across_z(sent):
        return lax.all_to_all(
            sent, "tm", split_axis=0, concat_axis=0, tiled=True, axis_index_groups=columns
        )

    barrier = lax.optimization_barrier
    plain = jnp.arange(NC, dtype=jnp.int32)
    mixed = jnp.bitwise_xor(plain, lax.axis_index("chan").astype(jnp.int32))
    own0 = spectra_of(0, records, alive, rows)
    own1 = spectra_apart(1, records, alive, rows, mixed)
    sent0 = lax.all_to_all(own0, "chan", split_axis=0, concat_axis=0, tiled=True)
    sent0, own1 = barrier((sent0, own1))
    planes0 = across_z(widen(sent0))
    slots1 = [own1[0]]
    for k in range(1, NC):
        slots1.append(lax.ppermute(own1[k], "chan", [(c, c ^ k) for c in range(NC)]))
    planes0, sent1 = barrier((planes0, arrange(mixed, slots1)))
    found0 = along_y(pack(place, planes0))
    planes1 = across_z(sent1).reshape(NZ, NY, GROUP, 2, WIN_DEV, BLOCK)
    down = [(i, i - NY) for i in range(NY, NZ * NY)]
    halo1 = lax.ppermute(planes1[:, :2], "tm", down)
    near1 = along_y(pack_groups(place, 0, 1, planes1))
    halo1, found0 = barrier((halo1, found0))
    next1 = along_y(pack_groups(place, 1, 1, planes1, halo1))
    result = stacks(relative, found0, 0, REACH)
    last1 = along_y(pack_groups(place, 2, 1, planes1, halo1))
    result = stacks(relative, near1 + next1, 1, 2 * GROUP, result)
    return last_stacks(relative, near1, last1, 1, result)


def solution(mesh):
    return jax.shard_map(
        per_device,
        mesh=mesh,
        in_specs=(P("tm", None, "chan"), P("chan"), P("tm", None)),
        out_specs=P("tm", None, "chan", None, None, None),
        check_vma=False,
    )
```

```python
import functools
import math

import jax
import jax.numpy as jnp
import numpy as np
from jax import lax
from jax.experimental import pallas as pl
from jax.experimental.pallas import tpu as pltpu
from jax.sharding import PartitionSpec as P

WINLEN = 100
NBIN = 16
BLOCK = 128
WIN_DEV = 16
WINDOWS = 512
PAIRS = 9
NZ, NY, NC = 8, 4, 8
NF = 2
GROUP = 4
REACH = 12
COLS = 512


def dft_rows():
    t = np.arange(WINLEN)
    bins = np.arange(NBIN) + 4
    angle = 2.0 * np.pi * bins[:, None] * t[None, :] / WINLEN
    table = np.stack([np.cos(angle), -np.sin(angle)], axis=1) * math.sqrt(2.0 / WINLEN)
    high = table.astype(jnp.bfloat16)
    low = (table - high.astype(np.float64)).astype(jnp.bfloat16)
    parts = np.stack([high, low]).astype(np.float32).reshape(2, NC, NF, 2, WINLEN)
    parts = parts.transpose(2, 1, 0, 3, 4)
    rows = parts[:, :, :, :, None, :, None] * np.eye(WIN_DEV, dtype=np.float32)[:, None, :]
    return rows.reshape(NF, NC, 4 * WIN_DEV, WINLEN * WIN_DEV).astype(jnp.bfloat16)


def spectra_body(records, alive, lhs, store):
    x = records[...]
    signal = x.astype(jnp.float32)
    power = jnp.sum(signal * signal, axis=0) * (1.0 / WINLEN)
    scale = alive[...].astype(jnp.float32) / jnp.sqrt(power + 1e-05)
    x = x.reshape(WINLEN * WIN_DEV, COLS)
    y = jnp.dot(lhs, x, preferred_element_type=jnp.float32)
    for k in range(NC):
        at = 4 * WIN_DEV * k
        value = y[at : at + 2 * WIN_DEV] + y[at + 2 * WIN_DEV : at + 4 * WIN_DEV]
        for p in range(2):
            scaled = (value[p * WIN_DEV : (p + 1) * WIN_DEV] * scale).astype(jnp.bfloat16)
            for b in range(COLS // BLOCK):
                store(k, b, p, scaled[:, b * BLOCK : (b + 1) * BLOCK])


def spectra_kernel(records, alive, rows, out):
    def store(k, b, p, part):
        out[k, b, p] = part

    spectra_body(records, alive, rows[0].reshape(NC * 4 * WIN_DEV, WINLEN * WIN_DEV), store)


def spectra_of(f, records, alive, rows):
    channels = records.shape[2]
    blocks, per = channels // BLOCK, COLS // BLOCK
    return pl.pallas_call(
        spectra_kernel,
        grid=(channels // COLS,),
        in_specs=[
            pl.BlockSpec((WINLEN, WIN_DEV, COLS), lambda n: (0, 0, n)),
            pl.BlockSpec((1, COLS), lambda n: (0, n)),
            pl.BlockSpec((1,) + rows.shape[1:], lambda n: (f, 0, 0, 0)),
        ],
        out_specs=pl.BlockSpec((NC, per, 2, WIN_DEV, BLOCK), lambda n: (0, n, 0, 0, 0)),
        out_shape=jax.ShapeDtypeStruct((NC, blocks, 2, WIN_DEV, BLOCK), jnp.bfloat16),
        compiler_params=pltpu.CompilerParams(vmem_limit_bytes=60 << 20),
        name="spectra",
    )(records, alive, rows)


def spectra_apart_kernel(order, records, alive, *refs):
    rows, outs = refs[:NC], refs[NC:]

    def store(k, b, p, part):
        outs[k][b, p] = part

    spectra_body(records, alive, jnp.concatenate([r[0, 0] for r in rows], axis=0), store)


def spectra_apart(f, records, alive, rows, order):
    channels = records.shape[2]
    blocks, per = channels // BLOCK, COLS // BLOCK
    grid_spec = pltpu.PrefetchScalarGridSpec(
        num_scalar_prefetch=1,
        grid=(channels // COLS,),
        in_specs=[
            pl.BlockSpec((WINLEN, WIN_DEV, COLS), lambda n, o: (0, 0, n)),
            pl.BlockSpec((1, COLS), lambda n, o: (0, n)),
        ]
        + [pl.BlockSpec((1, 1) + rows.shape[2:], lambda n, o, k=k: (f, o[k], 0, 0)) for k in range(NC)],
        out_specs=[pl.BlockSpec((per, 2, WIN_DEV, BLOCK), lambda n, o: (n, 0, 0, 0))] * NC,
    )
    return pl.pallas_call(
        spectra_apart_kernel,
        grid_spec=grid_spec,
        out_shape=[jax.ShapeDtypeStruct((blocks, 2, WIN_DEV, BLOCK), jnp.bfloat16)] * NC,
        compiler_params=pltpu.CompilerParams(vmem_limit_bytes=60 << 20),
        name="spectra",
    )(order, records, alive, *([rows] * NC))


def place_plane(out, plane, value):
    out[plane, :NY] = value
    out[lax.rem(plane + NZ - 1, NZ), NY:] = value[:2]


def widen_kernel(planes, out):
    for k in range(NZ):
        place_plane(out, k, planes[k])


def widen(planes):
    vmem = pl.BlockSpec(memory_space=pltpu.VMEM)
    return pl.pallas_call(
        widen_kernel,
        in_specs=[vmem],
        out_specs=vmem,
        out_shape=jax.ShapeDtypeStruct((NZ, NY + 2, GROUP, 2, WIN_DEV, BLOCK), jnp.bfloat16),
        compiler_params=pltpu.CompilerParams(vmem_limit_bytes=16 << 20),
        name="widen",
    )(planes.reshape(NZ, NY, GROUP, 2, WIN_DEV, BLOCK))


def arrange_kernel(order, *refs):
    for k in range(NC):
        refs[NC][order[k]] = refs[k][...]


def arrange(order, slots):
    vmem = pl.BlockSpec(memory_space=pltpu.VMEM)
    return pl.pallas_call(
        arrange_kernel,
        in_specs=[pl.BlockSpec(memory_space=pltpu.SMEM)] + [vmem] * NC,
        out_specs=vmem,
        out_shape=jax.ShapeDtypeStruct((NC,) + slots[0].shape, jnp.bfloat16),
        compiler_params=pltpu.CompilerParams(vmem_limit_bytes=16 << 20),
        name="arrange",
    )(order, *slots)


def pack_kernel(place, planes, *outs):
    for k in range(NY):
        outs[k][...] = planes[:, pl.ds(lax.rem(place[0] + k, NY), 3)]


def pack(place, planes):
    vmem = pl.BlockSpec(memory_space=pltpu.VMEM)
    shape = jax.ShapeDtypeStruct((NZ, 3, GROUP, 2, WIN_DEV, BLOCK), jnp.bfloat16)
    return pl.pallas_call(
        pack_kernel,
        in_specs=[pl.BlockSpec(memory_space=pltpu.SMEM), vmem],
        out_specs=[vmem] * NY,
        out_shape=[shape] * NY,
        compiler_params=pltpu.CompilerParams(vmem_limit_bytes=16 << 20),
        name="pack",
    )(place, planes)


def pack_group_kernel(first, place, planes, *refs):
    halo, outs = (None, refs) if first == 0 else (refs[0], refs[1:])
    for n, out in enumerate(outs):
        group = lax.rem(place[0] + n % NY, NY) + max(first, 0) + n // NY
        if first == 0:
            out[...] = planes[:, group]
        else:

            @pl.when(group < NY)
            def _():
                out[...] = planes[:, group]

            @pl.when(group >= NY)
            def _():
                out[...] = halo[:, group - NY]


def pack_groups(place, first, count, *sources):
    vmem = pl.BlockSpec(memory_space=pltpu.VMEM)
    shape = jax.ShapeDtypeStruct((NZ, GROUP, 2, WIN_DEV, BLOCK), jnp.bfloat16)
    return pl.pallas_call(
        functools.partial(pack_group_kernel, first),
        in_specs=[pl.BlockSpec(memory_space=pltpu.SMEM)] + [vmem] * len(sources),
        out_specs=[vmem] * (NY * count),
        out_shape=[shape] * (NY * count),
        compiler_params=pltpu.CompilerParams(vmem_limit_bytes=16 << 20),
        name="pack",
    )(place, *sources)


def real_and_imag(product):
    real = product[:BLOCK, :BLOCK] + product[BLOCK:, BLOCK:]
    imag = product[:BLOCK, BLOCK:] - product[BLOCK:, :BLOCK]
    inverse = 1.0 / math.sqrt(WINDOWS)
    return (real * inverse).astype(jnp.bfloat16), (imag * inverse).astype(jnp.bfloat16)


def fill(window, at, tiles, y, p):
    rows = NZ * WIN_DEV
    window[at, y * rows : (y + 1) * rows, p * BLOCK : (p + 1) * BLOCK] = tiles.reshape(rows, BLOCK)


def last_kernel(f, relative, *refs):
    near, last, out = refs[:NY], refs[NY : 2 * NY], refs[2 * NY + 1]
    window, own, staged, sems = refs[2 * NY + 2 :]
    for y in range(NY):
        for b in range(GROUP):
            for p in range(2):
                fill(own, b, near[y][:, b, p], y, p)
                fill(window, b, last[y][:, b, p], y, p)

    def each(step):
        for a in range(GROUP):
            for k in range(PAIRS):
                far = relative[a, k] - 2 * GROUP

                @pl.when(far >= 0)
                def _():
                    step(pltpu.make_async_copy(staged.at[a, far], out.at[a, k, f], sems.at[a, k]))

    for a in range(GROUP):
        own_t = own[a].T
        for b in range(a + 1):
            product = jnp.dot(own_t, window[b], preferred_element_type=jnp.float32)
            staged[a, b, 0], staged[a, b, 1] = real_and_imag(product)
    each(lambda copy: copy.start())
    each(lambda copy: copy.wait())


def last_stacks(relative, near, last, f, earlier):
    vmem = pl.BlockSpec(memory_space=pltpu.VMEM)
    blocks = pltpu.VMEM((GROUP, WINDOWS, 2 * BLOCK), jnp.bfloat16)
    return pl.pallas_call(
        functools.partial(last_kernel, f),
        in_specs=[pl.BlockSpec(memory_space=pltpu.SMEM)]
        + [vmem] * (2 * NY)
        + [pl.BlockSpec(memory_space=pl.ANY)],
        out_specs=pl.BlockSpec(memory_space=pl.ANY),
        out_shape=jax.ShapeDtypeStruct(earlier.shape, earlier.dtype),
        input_output_aliases={1 + 2 * NY: 0},
        scratch_shapes=[
            blocks,
            blocks,
            pltpu.VMEM((GROUP, GROUP, 2, BLOCK, BLOCK), jnp.bfloat16),
            pltpu.SemaphoreType.DMA((GROUP, PAIRS)),
        ],
        compiler_params=pltpu.CompilerParams(vmem_limit_bytes=20 << 20),
        name="last_stacks",
    )(relative, *near, *last, earlier)


def pairs_kernel(f, low, high, relative, *refs):
    sources, out = refs[:-5], refs[-5]
    window, staged, own_t, sems = refs[-4:]
    for y in range(NY):
        for b in range(high):
            for p in range(2):
                if sources[0].ndim == 6:
                    tiles = sources[y][:, b // GROUP, b % GROUP, p]
                else:
                    tiles = sources[b // GROUP * NY + y][:, b % GROUP, p]
                fill(window, b, tiles, y, p)

    def each(a, step):
        for k in range(PAIRS):
            partner = relative[a, k]

            @pl.when(jnp.logical_and(partner >= low, partner < high))
            def _():
                step(pltpu.make_async_copy(staged.at[a, partner - low], out.at[a, k, f], sems.at[a, k]))

    for a in range(GROUP):
        own_t[...] = window[a].T
        for b in range(max(low, a), min(high, a + PAIRS)):
            product = jnp.dot(own_t[...], window[b], preferred_element_type=jnp.float32)
            staged[a, b - low, 0], staged[a, b - low, 1] = real_and_imag(product)
        each(a, lambda copy: copy.start())
    for a in range(GROUP):
        each(a, lambda copy: copy.wait())


def pairs(relative, sources, f, low, high, earlier=None):
    vmem = pl.BlockSpec(memory_space=pltpu.VMEM)
    args = list(sources)
    specs = [vmem] * len(args)
    aliases = {}
    if earlier is not None:
        aliases = {1 + len(args): 0}
        args.append(earlier)
        specs.append(pl.BlockSpec(memory_space=pl.ANY))

    def kernel(relative, *refs):
        pairs_kernel(f, low, high, relative, *refs[: len(sources)], *refs[len(args) :])

    return pl.pallas_call(
        kernel,
        in_specs=[pl.BlockSpec(memory_space=pltpu.SMEM)] + specs,
        out_specs=pl.BlockSpec(memory_space=pl.ANY),
        out_shape=jax.ShapeDtypeStruct((GROUP, PAIRS, NF, 2, BLOCK, BLOCK), jnp.bfloat16),
        input_output_aliases=aliases,
        scratch_shapes=[
            pltpu.VMEM((high, WINDOWS, 2 * BLOCK), jnp.bfloat16),
            pltpu.VMEM((GROUP, high - low, 2, BLOCK, BLOCK), jnp.bfloat16),
            pltpu.VMEM((2 * BLOCK, WINDOWS), jnp.bfloat16),
            pltpu.SemaphoreType.DMA((GROUP, PAIRS)),
        ],
        compiler_params=pltpu.CompilerParams(vmem_limit_bytes=20 << 20),
        name="pairs",
    )(relative, *args)


def per_device(records, alive, partner):
    tm = lax.axis_index("tm")
    place = (tm % NY).reshape(1).astype(jnp.int32)
    relative = partner - tm * GROUP
    rows = jnp.asarray(dft_rows())
    records, alive = jnp.transpose(records, (1, 0, 2)), alive.reshape(1, -1)
    columns = [[z * NY + y for z in range(NZ)] for y in range(NY)]
    rounds = [[(i, i // NY * NY + (i + k) % NY) for i in range(NZ * NY)] for k in range(NY)]

    def along_y(packed):
        return [packed[0]] + [lax.ppermute(packed[k], "tm", rounds[k]) for k in range(1, NY)]

    def across_z(sent):
        return lax.all_to_all(
            sent, "tm", split_axis=0, concat_axis=0, tiled=True, axis_index_groups=columns
        )

    barrier = lax.optimization_barrier
    plain = jnp.arange(NC, dtype=jnp.int32)
    mixed = jnp.bitwise_xor(plain, lax.axis_index("chan").astype(jnp.int32))
    own0 = spectra_of(0, records, alive, rows)
    own1 = spectra_apart(1, records, alive, rows, mixed)
    sent0 = lax.all_to_all(own0, "chan", split_axis=0, concat_axis=0, tiled=True)
    sent0, own1 = barrier((sent0, own1))
    planes0 = across_z(widen(sent0))
    slots1 = [own1[0]]
    for k in range(1, NC):
        slots1.append(lax.ppermute(own1[k], "chan", [(c, c ^ k) for c in range(NC)]))
    planes0, sent1 = barrier((planes0, arrange(mixed, slots1)))
    found0 = along_y(pack(place, planes0))
    planes1 = across_z(sent1).reshape(NZ, NY, GROUP, 2, WIN_DEV, BLOCK)
    down = [(i, i - NY) for i in range(NY, NZ * NY)]
    halo1 = lax.ppermute(planes1[:, :2], "tm", down)
    near1 = along_y(pack_groups(place, 0, 1, planes1))
    halo1, found0 = barrier((halo1, found0))
    next1 = along_y(pack_groups(place, 1, 1, planes1, halo1))
    result = pairs(relative, found0, 0, 0, REACH)
    last1 = along_y(pack_groups(place, 2, 1, planes1, halo1))
    result = pairs(relative, near1 + next1, 1, 0, 2 * GROUP, result)
    return last_stacks(relative, near1, last1, 1, result)


def solution(mesh):
    return jax.shard_map(
        per_device,
        mesh=mesh,
        in_specs=(P("tm", None, "chan"), P("chan"), P("tm", None)),
        out_specs=P("tm", None, "chan", None, None, None),
        check_vma=False,
    )
```

```python
import functools
import math

import jax
import jax.numpy as jnp
import numpy as np
from jax import lax
from jax.experimental import pallas as pl
from jax.experimental.pallas import tpu as pltpu
from jax.sharding import PartitionSpec as P

WINLEN = 100
NBIN = 16
BLOCK = 128
WIN_DEV = 16
WINDOWS = 512
PAIRS = 9
NZ, NY, NC = 8, 4, 8
NF = 2
GROUP = 4
REACH = 12
COLS = 512


def dft_rows():
    t = np.arange(WINLEN)
    bins = np.arange(NBIN) + 4
    angle = 2.0 * np.pi * bins[:, None] * t[None, :] / WINLEN
    table = np.stack([np.cos(angle), -np.sin(angle)], axis=1) * math.sqrt(2.0 / WINLEN)
    high = table.astype(jnp.bfloat16)
    low = (table - high.astype(np.float64)).astype(jnp.bfloat16)
    parts = np.stack([high, low]).astype(np.float32).reshape(2, NC, NF, 2, WINLEN)
    parts = parts.transpose(2, 1, 0, 3, 4)
    rows = parts[:, :, :, :, None, :, None] * np.eye(WIN_DEV, dtype=np.float32)[:, None, :]
    return rows.reshape(NF, NC, 4 * WIN_DEV, WINLEN * WIN_DEV).astype(jnp.bfloat16)


def spectra_body(records, alive, lhs, store):
    x = records[...]
    signal = x.astype(jnp.float32)
    power = jnp.sum(signal * signal, axis=0) * (1.0 / WINLEN)
    scale = alive[...].astype(jnp.float32) / jnp.sqrt(power + 1e-05)
    x = x.reshape(WINLEN * WIN_DEV, COLS)
    y = jnp.dot(lhs, x, preferred_element_type=jnp.float32)
    for k in range(NC):
        at = 4 * WIN_DEV * k
        value = y[at : at + 2 * WIN_DEV] + y[at + 2 * WIN_DEV : at + 4 * WIN_DEV]
        for p in range(2):
            scaled = (value[p * WIN_DEV : (p + 1) * WIN_DEV] * scale).astype(jnp.bfloat16)
            for b in range(COLS // BLOCK):
                store(k, b, p, scaled[:, b * BLOCK : (b + 1) * BLOCK])


def spectra_kernel(records, alive, rows, out):
    def store(k, b, p, part):
        out[k, b, p] = part

    spectra_body(records, alive, rows[0].reshape(NC * 4 * WIN_DEV, WINLEN * WIN_DEV), store)


def spectra_of(f, records, alive, rows):
    channels = records.shape[2]
    blocks, per = channels // BLOCK, COLS // BLOCK
    return pl.pallas_call(
        spectra_kernel,
        grid=(channels // COLS,),
        in_specs=[
            pl.BlockSpec((WINLEN, WIN_DEV, COLS), lambda n: (0, 0, n)),
            pl.BlockSpec((1, COLS), lambda n: (0, n)),
            pl.BlockSpec((1,) + rows.shape[1:], lambda n: (f, 0, 0, 0)),
        ],
        out_specs=pl.BlockSpec((NC, per, 2, WIN_DEV, BLOCK), lambda n: (0, n, 0, 0, 0)),
        out_shape=jax.ShapeDtypeStruct((NC, blocks, 2, WIN_DEV, BLOCK), jnp.bfloat16),
        compiler_params=pltpu.CompilerParams(vmem_limit_bytes=60 << 20),
        name="spectra",
    )(records, alive, rows)


def spectra_apart_kernel(order, records, alive, *refs):
    rows, outs = refs[:NC], refs[NC:]

    def store(k, b, p, part):
        outs[k][b, p] = part

    spectra_body(records, alive, jnp.concatenate([r[0, 0] for r in rows], axis=0), store)


def spectra_apart(f, records, alive, rows, order):
    channels = records.shape[2]
    blocks, per = channels // BLOCK, COLS // BLOCK
    grid_spec = pltpu.PrefetchScalarGridSpec(
        num_scalar_prefetch=1,
        grid=(channels // COLS,),
        in_specs=[
            pl.BlockSpec((WINLEN, WIN_DEV, COLS), lambda n, o: (0, 0, n)),
            pl.BlockSpec((1, COLS), lambda n, o: (0, n)),
        ]
        + [pl.BlockSpec((1, 1) + rows.shape[2:], lambda n, o, k=k: (f, o[k], 0, 0)) for k in range(NC)],
        out_specs=[pl.BlockSpec((per, 2, WIN_DEV, BLOCK), lambda n, o: (n, 0, 0, 0))] * NC,
    )
    return pl.pallas_call(
        spectra_apart_kernel,
        grid_spec=grid_spec,
        out_shape=[jax.ShapeDtypeStruct((blocks, 2, WIN_DEV, BLOCK), jnp.bfloat16)] * NC,
        compiler_params=pltpu.CompilerParams(vmem_limit_bytes=60 << 20),
        name="spectra",
    )(order, records, alive, *([rows] * NC))


def place_plane(out, plane, value):
    out[plane, :NY] = value
    out[lax.rem(plane + NZ - 1, NZ), NY:] = value[:2]


def widen_kernel(planes, out):
    for k in range(NZ):
        place_plane(out, k, planes[k])


def widen(planes):
    vmem = pl.BlockSpec(memory_space=pltpu.VMEM)
    return pl.pallas_call(
        widen_kernel,
        in_specs=[vmem],
        out_specs=vmem,
        out_shape=jax.ShapeDtypeStruct((NZ, NY + 2, GROUP, 2, WIN_DEV, BLOCK), jnp.bfloat16),
        compiler_params=pltpu.CompilerParams(vmem_limit_bytes=16 << 20),
        name="widen",
    )(planes.reshape(NZ, NY, GROUP, 2, WIN_DEV, BLOCK))


def arrange_kernel(order, *refs):
    for k in range(NC):
        refs[NC][order[k]] = refs[k][...]


def arrange(order, slots):
    vmem = pl.BlockSpec(memory_space=pltpu.VMEM)
    return pl.pallas_call(
        arrange_kernel,
        in_specs=[pl.BlockSpec(memory_space=pltpu.SMEM)] + [vmem] * NC,
        out_specs=vmem,
        out_shape=jax.ShapeDtypeStruct((NC,) + slots[0].shape, jnp.bfloat16),
        compiler_params=pltpu.CompilerParams(vmem_limit_bytes=16 << 20),
        name="arrange",
    )(order, *slots)


def pack_kernel(place, planes, *outs):
    for k in range(NY):
        outs[k][...] = planes[:, pl.ds(lax.rem(place[0] + k, NY), 3)]


def pack(place, planes):
    vmem = pl.BlockSpec(memory_space=pltpu.VMEM)
    shape = jax.ShapeDtypeStruct((NZ, 3, GROUP, 2, WIN_DEV, BLOCK), jnp.bfloat16)
    return pl.pallas_call(
        pack_kernel,
        in_specs=[pl.BlockSpec(memory_space=pltpu.SMEM), vmem],
        out_specs=[vmem] * NY,
        out_shape=[shape] * NY,
        compiler_params=pltpu.CompilerParams(vmem_limit_bytes=16 << 20),
        name="pack",
    )(place, planes)


def pack_group_kernel(first, place, planes, *refs):
    halo, outs = (None, refs) if first == 0 else (refs[0], refs[1:])
    for n, out in enumerate(outs):
        group = lax.rem(place[0] + n % NY, NY) + max(first, 0) + n // NY
        if first == 0:
            out[...] = planes[:, group]
        else:

            @pl.when(group < NY)
            def _():
                out[...] = planes[:, group]

            @pl.when(group >= NY)
            def _():
                out[...] = halo[:, group - NY]


def pack_groups(place, first, count, *sources):
    vmem = pl.BlockSpec(memory_space=pltpu.VMEM)
    shape = jax.ShapeDtypeStruct((NZ, GROUP, 2, WIN_DEV, BLOCK), jnp.bfloat16)
    return pl.pallas_call(
        functools.partial(pack_group_kernel, first),
        in_specs=[pl.BlockSpec(memory_space=pltpu.SMEM)] + [vmem] * len(sources),
        out_specs=[vmem] * (NY * count),
        out_shape=[shape] * (NY * count),
        compiler_params=pltpu.CompilerParams(vmem_limit_bytes=16 << 20),
        name="pack",
    )(place, *sources)


def real_and_imag(product):
    real = product[:BLOCK, :BLOCK] + product[BLOCK:, BLOCK:]
    imag = product[:BLOCK, BLOCK:] - product[BLOCK:, :BLOCK]
    inverse = 1.0 / math.sqrt(WINDOWS)
    return (real * inverse).astype(jnp.bfloat16), (imag * inverse).astype(jnp.bfloat16)


def fill(window, at, tiles, y, p):
    rows = NZ * WIN_DEV
    window[at, y * rows : (y + 1) * rows, p * BLOCK : (p + 1) * BLOCK] = tiles.reshape(rows, BLOCK)


def last_kernel(f, relative, *refs):
    own_t, last, out = refs[0], refs[1 : NY + 1], refs[NY + 2]
    window, staged, sems = refs[NY + 3 :]
    for y in range(NY):
        for b in range(GROUP):
            for p in range(2):
                fill(window, b, last[y][:, b, p], y, p)

    def each(step):
        for a in range(GROUP):
            for k in range(PAIRS):
                far = relative[a, k] - 2 * GROUP

                @pl.when(far >= 0)
                def _():
                    step(pltpu.make_async_copy(staged.at[a, far], out.at[a, k, f], sems.at[a, k]))

    for a in range(GROUP):
        for b in range(a + 1):
            product = jnp.dot(own_t[a], window[b], preferred_element_type=jnp.float32)
            staged[a, b, 0], staged[a, b, 1] = real_and_imag(product)
    each(lambda copy: copy.start())
    each(lambda copy: copy.wait())


def last_stacks(relative, own_t, last, f, earlier):
    vmem = pl.BlockSpec(memory_space=pltpu.VMEM)
    blocks = pltpu.VMEM((GROUP, WINDOWS, 2 * BLOCK), jnp.bfloat16)
    return pl.pallas_call(
        functools.partial(last_kernel, f),
        in_specs=[pl.BlockSpec(memory_space=pltpu.SMEM)]
        + [vmem] * (NY + 1)
        + [pl.BlockSpec(memory_space=pl.ANY)],
        out_specs=pl.BlockSpec(memory_space=pl.ANY),
        out_shape=jax.ShapeDtypeStruct(earlier.shape, earlier.dtype),
        input_output_aliases={2 + NY: 0},
        scratch_shapes=[
            blocks,
            pltpu.VMEM((GROUP, GROUP, 2, BLOCK, BLOCK), jnp.bfloat16),
            pltpu.SemaphoreType.DMA((GROUP, PAIRS)),
        ],
        compiler_params=pltpu.CompilerParams(vmem_limit_bytes=20 << 20),
        name="last_stacks",
    )(relative, own_t, *last, earlier)


def pairs_kernel(f, low, high, relative, *refs):
    sources, out, own_t = refs[:-5], refs[-5], refs[-4]
    window, staged, sems = refs[-3:]
    for y in range(NY):
        for b in range(high):
            for p in range(2):
                if sources[0].ndim == 6:
                    tiles = sources[y][:, b // GROUP, b % GROUP, p]
                else:
                    tiles = sources[b // GROUP * NY + y][:, b % GROUP, p]
                fill(window, b, tiles, y, p)

    def each(a, step):
        for k in range(PAIRS):
            partner = relative[a, k]

            @pl.when(jnp.logical_and(partner >= low, partner < high))
            def _():
                step(pltpu.make_async_copy(staged.at[a, partner - low], out.at[a, k, f], sems.at[a, k]))

    for a in range(GROUP):
        own_t[a] = window[a].T
        for b in range(max(low, a), min(high, a + PAIRS)):
            product = jnp.dot(own_t[a], window[b], preferred_element_type=jnp.float32)
            staged[a, b - low, 0], staged[a, b - low, 1] = real_and_imag(product)
        each(a, lambda copy: copy.start())
    for a in range(GROUP):
        each(a, lambda copy: copy.wait())


def pairs(relative, sources, f, low, high, earlier=None):
    vmem = pl.BlockSpec(memory_space=pltpu.VMEM)
    args = list(sources)
    specs = [vmem] * len(args)
    aliases = {}
    if earlier is not None:
        aliases = {1 + len(args): 0}
        args.append(earlier)
        specs.append(pl.BlockSpec(memory_space=pl.ANY))

    def kernel(relative, *refs):
        pairs_kernel(f, low, high, relative, *refs[: len(sources)], *refs[len(args) :])

    return pl.pallas_call(
        kernel,
        in_specs=[pl.BlockSpec(memory_space=pltpu.SMEM)] + specs,
        out_specs=[pl.BlockSpec(memory_space=pl.ANY), vmem],
        out_shape=[
            jax.ShapeDtypeStruct((GROUP, PAIRS, NF, 2, BLOCK, BLOCK), jnp.bfloat16),
            jax.ShapeDtypeStruct((GROUP, 2 * BLOCK, WINDOWS), jnp.bfloat16),
        ],
        input_output_aliases=aliases,
        scratch_shapes=[
            pltpu.VMEM((high, WINDOWS, 2 * BLOCK), jnp.bfloat16),
            pltpu.VMEM((GROUP, high - low, 2, BLOCK, BLOCK), jnp.bfloat16),
            pltpu.SemaphoreType.DMA((GROUP, PAIRS)),
        ],
        compiler_params=pltpu.CompilerParams(vmem_limit_bytes=20 << 20),
        name="pairs",
    )(relative, *args)


def per_device(records, alive, partner):
    tm = lax.axis_index("tm")
    place = (tm % NY).reshape(1).astype(jnp.int32)
    relative = partner - tm * GROUP
    rows = jnp.asarray(dft_rows())
    records, alive = jnp.transpose(records, (1, 0, 2)), alive.reshape(1, -1)
    columns = [[z * NY + y for z in range(NZ)] for y in range(NY)]
    rounds = [[(i, i // NY * NY + (i + k) % NY) for i in range(NZ * NY)] for k in range(NY)]

    def along_y(packed):
        return [packed[0]] + [lax.ppermute(packed[k], "tm", rounds[k]) for k in range(1, NY)]

    def across_z(sent):
        return lax.all_to_all(
            sent, "tm", split_axis=0, concat_axis=0, tiled=True, axis_index_groups=columns
        )

    barrier = lax.optimization_barrier
    plain = jnp.arange(NC, dtype=jnp.int32)
    mixed = jnp.bitwise_xor(plain, lax.axis_index("chan").astype(jnp.int32))
    own0 = spectra_of(0, records, alive, rows)
    own1 = spectra_apart(1, records, alive, rows, mixed)
    sent0 = lax.all_to_all(own0, "chan", split_axis=0, concat_axis=0, tiled=True)
    sent0, own1 = barrier((sent0, own1))
    planes0 = across_z(widen(sent0))
    slots1 = [own1[0]]
    for k in range(1, NC):
        slots1.append(lax.ppermute(own1[k], "chan", [(c, c ^ k) for c in range(NC)]))
    planes0, sent1 = barrier((planes0, arrange(mixed, slots1)))
    found0 = along_y(pack(place, planes0))
    planes1 = across_z(sent1).reshape(NZ, NY, GROUP, 2, WIN_DEV, BLOCK)
    down = [(i, i - NY) for i in range(NY, NZ * NY)]
    halo1 = lax.ppermute(planes1[:, :2], "tm", down)
    near1 = along_y(pack_groups(place, 0, 1, planes1))
    halo1, found0 = barrier((halo1, found0))
    next1 = along_y(pack_groups(place, 1, 1, planes1, halo1))
    result, _ = pairs(relative, found0, 0, 0, REACH)
    last1 = along_y(pack_groups(place, 2, 1, planes1, halo1))
    result, own_t = pairs(relative, near1 + next1, 1, 0, 2 * GROUP, result)
    return last_stacks(relative, own_t, last1, 1, result)


def solution(mesh):
    return jax.shard_map(
        per_device,
        mesh=mesh,
        in_specs=(P("tm", None, "chan"), P("chan"), P("tm", None)),
        out_specs=P("tm", None, "chan", None, None, None),
        check_vma=False,
    )
```
